32 devices in a mesh: row: 8 (over z, y), col: 4 (over x, core).
Axes of the slice: x: 2, y: 2, z: 4, core: 2. Of those that a mesh axis runs over, the one named last changes fastest.
Arguments:
- matrix: float32 [18432, 18432], P('row', 'col'), as said below
Outputs:
- updated: float32 [18432, 18432], P('row', 'col')
- reflectors: float32 [18432, 512], P('row')
Inputs may be any that keep to these rules, and one draw needn't show every extreme that they name: matrix is symmetric.
All inputs are finite; a program needn't handle non-finite values.
Results may differ from the reference program's by a relative error of at most 0.00016.
Values sent between devices are 32-bit elements; how exact they have to be, the bound alone decides.
No kernel may reach another device: no remote copies, remote signals or barrier semaphores. Data moves between devices by JAX's collectives and lax.ppermute only.
A program may use at most 256 MiB of HBM per device.

```python
import jax
import jax.numpy as jnp
from jax import lax

NMAT = 18432
BAND = 256
PANELS = 2


def draw_matrix(key, part):
    first_key = jax.random.fold_in(key, 0)
    third_key = jax.random.fold_in(key, 2)
    random_part = jax.random.normal(first_key, (NMAT, NMAT), jnp.float32)
    planted = jax.random.normal(third_key, (2, BAND, BAND), jnp.float32)
    random_part = (random_part + random_part.T) * 0.7071
    planted = (planted + jnp.swapaxes(planted, 1, 2)) * 0.7071
    strength = 0.8 * jnp.sqrt(jnp.float32(NMAT))
    spread = 0.4 / jnp.sqrt(jnp.float32(BAND))
    unit_block = jnp.eye(BAND, dtype=jnp.float32)
    first_block = strength * (unit_block + spread * planted[0])
    second_block = -strength * (unit_block + spread * planted[1])
    empty_block = jnp.zeros((BAND, BAND), jnp.float32)
    upper_rows = jnp.concatenate([empty_block, first_block, empty_block], axis=1)
    middle_rows = jnp.concatenate([first_block, empty_block, second_block], axis=1)
    lower_rows = jnp.concatenate([empty_block, second_block, empty_block], axis=1)
    corner = jnp.concatenate([upper_rows, middle_rows, lower_rows], axis=0)
    rest = NMAT - 3 * BAND
    placed = jnp.pad(corner, ((0, rest), (0, rest)))
    return (random_part + placed).astype(jnp.float32)


def setup_inputs(seed: int = 0) -> dict:
    key_of = jax.random.split(jax.random.key(seed), 2)
    return {
        "matrix": draw_matrix(jax.random.fold_in(key_of[1], 71), 0),
    }


def reference(matrix):
    current = matrix
    positions = jnp.arange(NMAT, dtype=jnp.int32)
    columns = jnp.arange(BAND, dtype=jnp.int32)
    identity = jnp.eye(BAND, dtype=jnp.float32)
    high = lax.Precision.HIGHEST
    stored = []
    for which_panel in range(PANELS):
        start = (which_panel + 1) * BAND
        panel_rows = jnp.where(positions[:, None] >= start, current[:, which_panel * BAND:(which_panel + 1) * BAND], 0.0)
        unit_rows = (positions[:, None] - start == columns[None, :]).astype(jnp.float32)
        gram_sum = jnp.dot(panel_rows.T, panel_rows, precision=high)
        top_block = jnp.dot(unit_rows.T, panel_rows, precision=high)
        factor_low = jnp.linalg.cholesky(gram_sum)
        q_rows = jax.scipy.linalg.solve_triangular(factor_low, panel_rows.T, lower=True).T
        q_top = jax.scipy.linalg.solve_triangular(factor_low, top_block.T, lower=True).T
        shifted = identity + q_top
        factor_two = jnp.linalg.cholesky(jnp.dot(shifted, shifted.T, precision=high))
        inner = jax.scipy.linalg.solve_triangular(factor_two, identity, lower=True)
        transform = jnp.dot(shifted.T, jnp.dot(inner.T, inner, precision=high), precision=high)
        vectors = q_rows + unit_rows
        stored.append(vectors)
        image = jnp.dot(current, vectors, precision=high)
        curvature = jnp.dot(vectors.T, image, precision=high)
        middle = jnp.dot(jnp.dot(transform, curvature, precision=high), transform.T, precision=high)
        w_full = jnp.dot(image, transform.T, precision=high) - 0.5 * jnp.dot(vectors, middle, precision=high)
        current = current - jnp.dot(vectors, w_full.T, precision=high) - jnp.dot(w_full, vectors.T, precision=high)
    return (current, jnp.concatenate(stored, axis=1))
```

```python
import functools

import jax
import jax.numpy as jnp
from jax import lax
from jax.experimental import pallas as pl
from jax.experimental.pallas import tpu as pltpu
from jax.sharding import PartitionSpec as P

BAND = 256
NB = 64
EXACT = lax.Precision.HIGHEST


def dot_in(left, right, dims=((1,), (0,))):
    return lax.dot_general(
        left, right, (dims, ((), ())), precision=EXACT, preferred_element_type=jnp.float32
    )


def beside_identity(block):
    size = block.shape[0]
    rows = lax.broadcasted_iota(jnp.int32, (size, size), 0)
    columns = lax.broadcasted_iota(jnp.int32, (size, size), 1)
    return jnp.concatenate([block, (rows == columns).astype(jnp.float32)], axis=1)


def eliminate_below(both):
    size = both.shape[0]
    tiles = [both[8 * i : 8 * i + 8] for i in range(size // 8)]
    place = lax.broadcasted_iota(jnp.int32, (8, 2 * size), 0)
    for k in range(size):
        first, inside = divmod(k, 8)
        row = tiles[first][inside : inside + 1, :]
        scale = lax.rsqrt(row[:, k : k + 1])
        scaled = row * scale
        twice = scaled * scale
        for b in range(first, len(tiles)):
            new = tiles[b] - tiles[b][:, k : k + 1] * twice
            if b == first:
                new = jnp.where(place > inside, new, jnp.where(place == inside, scaled, tiles[b]))
            tiles[b] = new
    return jnp.concatenate(tiles, axis=0)


def eliminate_all(both):
    size = both.shape[0]
    tiles = [both[8 * i : 8 * i + 8] for i in range(size // 8)]
    place = lax.broadcasted_iota(jnp.int32, (8, 2 * size), 0)
    for k in range(size):
        first, inside = divmod(k, 8)
        row = tiles[first][inside : inside + 1, :]
        scaled = row / row[:, k : k + 1]
        new_tiles = []
        for b in range(len(tiles)):
            new = tiles[b] - tiles[b][:, k : k + 1] * scaled
            if b == first:
                new = jnp.where(place == inside, scaled, new)
            new_tiles.append(new)
        tiles = new_tiles
    return jnp.concatenate(tiles, axis=0)


def square_places():
    rows = lax.broadcasted_iota(jnp.int32, (BAND, BAND), 0)
    columns = lax.broadcasted_iota(jnp.int32, (BAND, BAND), 1)
    return rows, columns


def factor_kernel(at, start_ref, out_ref, *scratch):
    work_ref = scratch[0] if scratch else out_ref
    rows, columns = square_places()
    if at == 0:
        work_ref[:, :BAND] = start_ref[...]
        work_ref[:, BAND:] = (rows == columns).astype(jnp.float32)
    else:
        work_ref[...] = start_ref[...]
    end = at + NB
    both = eliminate_below(beside_identity(work_ref[at:end, at:end]))
    strip = dot_in(both[:, NB:], work_ref[at:end, :])
    work_ref[at:end, :] = strip
    if end < BAND:
        work_ref[end:, :] -= dot_in(strip[:, end:BAND], strip, ((0,), (0,)))
    else:
        out_ref[...] = jnp.where(rows >= columns, work_ref[:, BAND:], 0.0)


def transform_kernel(at, *refs):
    if at == 0:
        top_ref, inverse_ref, out_ref = refs
        rows, columns = square_places()
        identity = (rows == columns).astype(jnp.float32)
        work_ref = out_ref
        work_ref[:, :BAND] = identity + dot_in(top_ref[...], inverse_ref[...], ((1,), (1,)))
        work_ref[:, BAND:] = identity
    else:
        start_ref, out_ref = refs[:2]
        work_ref = refs[2] if len(refs) > 2 else out_ref
        work_ref[...] = start_ref[...]
    end = at + NB
    both = eliminate_all(beside_identity(work_ref[at:end, at:end]))
    strip = dot_in(both[:, NB:], work_ref[at:end, :])
    if at > 0:
        work_ref[:at, :] -= dot_in(work_ref[:at, at:end], strip)
    if end < BAND:
        work_ref[end:, :] -= dot_in(work_ref[end:, at:end], strip)
    work_ref[at:end, :] = strip
    if end == BAND:
        out_ref[...] = work_ref[:, BAND:]


def by_steps(kernel, name, *operands):
    for at in range(0, BAND, NB):
        last = at + NB == BAND
        shape = (BAND, BAND) if last else (BAND, 2 * BAND)
        operands = (
            pl.pallas_call(
                functools.partial(kernel, at),
                out_shape=jax.ShapeDtypeStruct(shape, jnp.float32),
                scratch_shapes=[pltpu.VMEM((BAND, 2 * BAND), jnp.float32)] if last else [],
                cost_estimate=pl.CostEstimate(
                    flops=6 * 10**9, bytes_accessed=4 * 10**6, transcendentals=BAND
                ),
                name=name,
            )(*operands),
        )
    return operands[0]


NN, NT, TN = ((1,), (0,)), ((1,), (1,)), ((0,), (0,))
GRANT = 56 * 2**20


def halves(value):
    high = value.astype(jnp.bfloat16)
    return high, (value - high.astype(jnp.float32)).astype(jnp.bfloat16)


def dot1(left, right, dims):
    return lax.dot_general(left, right, (dims, ((), ())), preferred_element_type=jnp.float32)


def dot3(left, right, dims):
    lh, ll = halves(left)
    rh, rl = halves(right)
    return dot1(lh, rh, dims) + (dot1(lh, rl, dims) + dot1(ll, rh, dims))


def places_of(offset_ref, size):
    at = offset_ref[0] + pl.program_id(0) * size
    return at + lax.broadcasted_iota(jnp.int32, (size, BAND), 0)


def unit_of(places, start):
    columns = lax.broadcasted_iota(jnp.int32, places.shape, 1)
    return (places - start == columns).astype(jnp.float32)


def add_to(ref, value):
    @pl.when(pl.program_id(0) == 0)
    def _():
        ref[...] = value

    @pl.when(pl.program_id(0) > 0)
    def _():
        ref[...] += value


def first_kernel(offset_ref, raw_ref, image_ref, next_ref, inv_ref, y_ref, x_ref, mid_ref):
    places = places_of(offset_ref, raw_ref.shape[0])
    panel = jnp.where(places >= BAND, raw_ref[...], 0.0)
    y = dot3(panel, inv_ref[...], NT) + unit_of(places, BAND)
    x = dot3(image_ref[...], inv_ref[...], NT) + next_ref[...]
    y_ref[...] = y
    x_ref[...] = x
    add_to(mid_ref, dot3(y, x, TN))


def curvature(tm_ref, mid_ref):
    return dot3(dot3(tm_ref[...], mid_ref[...], NN), tm_ref[...], NT)


def second_kernel(
    offset_ref, y_ref, x_ref, next_ref, tm_ref, mid_ref, xh_ref, top_ref, inv_ref, w_ref, panel_ref, wh_ref, gram_ref, inner_ref
):
    places = places_of(offset_ref, y_ref.shape[0])
    s = curvature(tm_ref, mid_ref)
    rows, columns = square_places()
    yh = dot3(top_ref[...], inv_ref[...], NT) + (rows == columns).astype(F32)
    wh = dot3(xh_ref[...], tm_ref[...], NT) - 0.5 * dot3(yh, s, NN)
    y = y_ref[...]
    w = dot3(x_ref[...], tm_ref[...], NT) - 0.5 * dot3(y, s, NN)
    w_ref[...] = w
    panel = next_ref[...] - dot3(y, wh, NT) - dot3(w, yh, NT)
    panel_ref[...] = panel
    wh_ref[...] = wh
    panel = jnp.where(places >= 2 * BAND, panel, 0.0)
    add_to(gram_ref, dot_in(panel, panel, TN))
    add_to(inner_ref, jnp.concatenate([dot3(w, panel, TN), dot3(y, panel, TN)], axis=0))


def vectors_kernel(start, offset_ref, panel_ref, inv_ref, y_ref):
    places = places_of(offset_ref, panel_ref.shape[0])
    panel = jnp.where(places >= start, panel_ref[...], 0.0)
    y_ref[...] = dot3(panel, inv_ref[...], NT) + unit_of(places, start)


def halves_kernel(offset_ref, panel_ref, high_ref, low_ref):
    places = places_of(offset_ref, panel_ref.shape[0])
    high_ref[...], low_ref[...] = halves(jnp.where(places >= 2 * BAND, panel_ref[...], 0.0))


def sides_kernel(offset_ref, raw_ref, next_ref, panel_ref, inv_ref, tm_ref, wh_ref, y_ref, w_ref):
    places = places_of(offset_ref, raw_ref.shape[0])
    raw = jnp.where(places >= BAND, raw_ref[...], 0.0)
    y = dot3(raw, inv_ref[...], NT) + unit_of(places, BAND)
    y_ref[...] = y
    w_ref[...] = dot3(next_ref[...] - panel_ref[...] - dot3(y, wh_ref[...], NT), tm_ref[...], NT)


def last_kernel(y_ref, x_ref, tm_ref, mid_ref, w_ref):
    s = curvature(tm_ref, mid_ref)
    w_ref[...] = dot3(x_ref[...], tm_ref[...], NT) - 0.5 * dot3(y_ref[...], s, NN)


def gram_kernel(offset_ref, raw_ref, gram_ref, high_ref, low_ref):
    panel = jnp.where(places_of(offset_ref, raw_ref.shape[0]) >= BAND, raw_ref[...], 0.0)
    high_ref[...], low_ref[...] = halves(panel)
    add_to(gram_ref, dot_in(panel, panel, TN))


def next_kernel(
    offset_ref, raw_ref, y_ref, w_ref, wn_ref, low_ref, inv_ref, image_ref, inner_ref, panel_ref, new_ref, out_ref, v_ref, mid_ref
):
    y, w = y_ref[...], w_ref[...]
    yn = dot3(low_ref[...], inv_ref[...], NT)
    third = raw_ref[...] - dot3(y, wn_ref[...], NT) - dot3(w, yn, NT)
    image = image_ref[...] - dot3(y, inner_ref[:BAND], NN) - dot3(w, inner_ref[BAND:], NN)
    out = dot3(image, new_ref[...], NT) + third
    places = places_of(offset_ref, y.shape[0])
    panel = jnp.where(places >= 2 * BAND, panel_ref[...], 0.0)
    v = dot3(panel, new_ref[...], NT) + unit_of(places, 2 * BAND)
    out_ref[...] = out
    v_ref[...] = v
    add_to(mid_ref, dot3(v, out, TN))


F32, BF16 = jnp.float32, jnp.bfloat16


def by_rows(kernel, name, rows, operands, outs, flops):
    tile = rows // 4 if rows > 1000 and rows % 64 == 0 else rows

    def spec(shape):
        if shape[0] == rows:
            return pl.BlockSpec((tile, shape[1]), lambda i: (i, 0))
        return pl.BlockSpec(shape, lambda i: (0,) * len(shape))

    in_specs = [
        pl.BlockSpec(memory_space=pltpu.SMEM) if v.dtype == jnp.int32 else spec(v.shape) for v in operands
    ]
    shapes = [
        jax.ShapeDtypeStruct(o, F32) if isinstance(o, tuple) else jax.ShapeDtypeStruct((rows, BAND), o)
        for o in outs
    ]
    return pl.pallas_call(
        kernel,
        grid=(rows // tile,),
        in_specs=in_specs,
        out_specs=[spec(shape.shape) for shape in shapes],
        out_shape=shapes,
        compiler_params=pltpu.CompilerParams(vmem_limit_bytes=GRANT),
        cost_estimate=pl.CostEstimate(
            flops=flops * 12 * rows * BAND * BAND, bytes_accessed=4 * rows * BAND * 6, transcendentals=0
        ),
        name=name,
    )(*operands)


def image_kernel(matrix_ref, high_ref, low_ref, out_ref):
    high_panel = high_ref[...]
    both = jnp.concatenate([high_panel, low_ref[...]], axis=1)
    m = matrix_ref.shape[0]
    step = m // 4

    def part(at):
        high, low = halves(matrix_ref[at : at + step, :])
        wide = dot1(high, both, NN)
        return wide[:, :BAND] + (wide[:, BAND:] + dot1(low, high_panel, NN))

    @pl.when(pl.program_id(0) == 0)
    def _():
        for at in range(0, m, step):
            out_ref[at : at + step, :] = part(at)

    @pl.when(pl.program_id(0) > 0)
    def _():
        for at in range(0, m, step):
            out_ref[at : at + step, :] += part(at)


def image_of(matrix, high, low):
    m, n = matrix.shape
    deep = 512 if n % 512 == 0 else 256
    return pl.pallas_call(
        image_kernel,
        grid=(n // deep,),
        in_specs=[
            pl.BlockSpec((m, deep), lambda i: (0, i)),
            pl.BlockSpec((deep, BAND), lambda i: (i, 0)),
            pl.BlockSpec((deep, BAND), lambda i: (i, 0)),
        ],
        out_specs=pl.BlockSpec((m, BAND), lambda i: (0, 0)),
        out_shape=jax.ShapeDtypeStruct((m, BAND), F32),
        compiler_params=pltpu.CompilerParams(vmem_limit_bytes=GRANT),
        cost_estimate=pl.CostEstimate(
            flops=8 * m * n * BAND, bytes_accessed=4 * m * n, transcendentals=0
        ),
        name="image",
    )(matrix, high, low)


def update_kernel(matrix_ref, yr_ref, wr_ref, yc_ref, wc_ref, *rest):
    out_ref, high_ref, low_ref = rest[-3:]

    @pl.when(pl.program_id(0) == 0)
    def _():
        high_ref[:, :BAND], low_ref[:, :BAND] = halves(yr_ref[...])
        high_ref[:, BAND:], low_ref[:, BAND:] = halves(wr_ref[...])

    rh, rl = halves(jnp.concatenate([wc_ref[...], yc_ref[...]], axis=1))
    m = matrix_ref.shape[0]
    step = m // 4
    for at in range(0, m, step):
        part = slice(at, at + step)
        high, low = high_ref[part, :], low_ref[part, :]
        product = dot1(high, rh, NT) + (dot1(high, rl, NT) + dot1(low, rh, NT))
        out_ref[part, :] = matrix_ref[part, :] - product


def update(matrix, y_r, w_r, y_c, w_c, name, parts=1):
    m, n = matrix.shape
    wide = 512 if n % 512 == 0 else n // 9 if n % (9 * 128) == 0 else n
    blocks = n // wide
    parts = parts if blocks % parts == 0 else 1
    each = blocks // parts
    out = None
    for part in range(parts):
        here = functools.partial(lambda first, i: (0, first + i), part * each)
        down = functools.partial(lambda first, i: (first + i, 0), part * each)
        whole = pl.BlockSpec((m, BAND), lambda i: (0, 0), pipeline_mode=pl.Buffered(1))
        specs = [pl.BlockSpec((m, wide), here), whole, whole]
        specs += [pl.BlockSpec((wide, BAND), down)] * 2
        operands = [matrix, y_r, w_r, y_c, w_c]
        if out is not None:
            specs.append(pl.BlockSpec(memory_space=pl.ANY))
            operands.append(out)
        out = pl.pallas_call(
            update_kernel,
            grid=(each,),
            in_specs=specs,
            out_specs=pl.BlockSpec((m, wide), here),
            out_shape=jax.ShapeDtypeStruct((m, n), F32),
            scratch_shapes=[pltpu.VMEM((m, 2 * BAND), BF16)] * 2,
            input_output_aliases={5: 0} if len(operands) > 5 else {},
            compiler_params=pltpu.CompilerParams(vmem_limit_bytes=GRANT),
            cost_estimate=pl.CostEstimate(
                flops=16 * m * n * BAND // parts, bytes_accessed=8 * m * n // parts, transcendentals=0
            ),
            name=name,
        )(*operands)
    return out


class Moves:
    def __init__(self, mesh):
        self.rows = mesh.shape["row"]
        self.cols = mesh.shape["col"]
        self.per = self.rows // self.cols
        self.row = lax.axis_index("row")
        self.col = lax.axis_index("col")
        self.group = self.row // self.per
        self.lane = self.row % self.per

    def over_col(self, value, to):
        return lax.ppermute(value, "col", [(c, to(c)) for c in range(self.cols) if to(c) is not None])

    def over_both(self, value, pairs):
        flat = [(a * self.cols + b, d * self.cols + e) for (a, b), (d, e) in pairs]
        return lax.ppermute(value, ("row", "col"), flat)

    def spread(self, value):
        bit = self.cols // 2
        while bit:
            got = self.over_col(value, lambda c: c + bit if c % (2 * bit) == 0 else None)
            value = jnp.where(self.col % (2 * bit) == bit, got, value)
            bit //= 2
        return value

    def total(self, value):
        bit = 1
        while bit < self.cols:
            value = value + self.over_col(value, lambda c: c ^ bit)
            bit *= 2
        return value

    def bits(self):
        return [1 << i for i in range(self.cols.bit_length() - 1)]

    def scatter_sum(self, value):
        bits = self.bits()
        value = value.reshape(*[2] * len(bits), value.shape[0] // self.cols, value.shape[1])
        for bit in bits:
            axis = value.ndim - 3
            odd = (self.col // bit) % 2 == 1
            first = lax.index_in_dim(value, 0, axis, keepdims=False)
            second = lax.index_in_dim(value, 1, axis, keepdims=False)
            keep, give = jnp.where(odd, second, first), jnp.where(odd, first, second)
            value = keep + self.over_col(give, lambda c: c ^ bit)
        return value

    def collect(self, piece):
        for bit in self.bits()[::-1]:
            other = self.over_col(piece, lambda c: c ^ bit)
            odd = (self.col // bit) % 2 == 1
            piece = jnp.stack([jnp.where(odd, other, piece), jnp.where(odd, piece, other)], axis=-3)
        return piece.reshape(-1, piece.shape[-1])

    def over_row(self, value, to):
        return lax.ppermute(value, "row", [(r, to(r)) for r in range(self.rows)])

    def sum_all(self, value):
        half = value.shape[0] // 2
        odd = self.col % 2 == 1
        keep = jnp.where(odd, value[half:], value[:half])
        keep = keep + self.over_col(jnp.where(odd, value[:half], value[half:]), lambda c: c ^ 1)
        for bit in self.bits()[1:]:
            keep = keep + self.over_col(keep, lambda c: c ^ bit)
        for bit in [1 << i for i in range(self.rows.bit_length() - 1)]:
            keep = keep + self.over_row(keep, lambda r: r ^ bit)
        other = self.over_col(keep, lambda c: c ^ 1)
        return jnp.concatenate([jnp.where(odd, other, keep), jnp.where(odd, keep, other)], axis=0)

    def deal(self, value):
        size = value.shape[0] // self.cols
        piece = value[:size]
        for q in range(1, self.cols):
            got = self.over_col(value[q * size : (q + 1) * size], lambda c: q if c == 0 else None)
            piece = jnp.where(self.col == q, got, piece)
        return piece

    def rows_at(self, piece, first):
        size = piece.shape[0]
        mine = (self.row * self.cols + self.col) * size
        padded = jnp.pad(piece, ((BAND, BAND), (0, 0)))
        at = jnp.clip(first - mine + BAND, 0, size + BAND)
        return lax.dynamic_slice_in_dim(padded, at, BAND, axis=0)

    def place(self, piece):
        pairs = [
            ((g * self.per + y, q), (q * self.per + y, g))
            for g in range(self.cols)
            for y in range(self.per)
            for q in range(self.cols)
        ]
        return self.over_both(piece, pairs)

    def line(self, value):
        count = self.cols
        up, down = [value], [value]
        for step in range(count - 1):
            rising = range(step, count - 1)
            for parts, move in ((up, 1), (down, -1)):
                pairs = [
                    (g * self.per + y, (g + move) * self.per + y)
                    for g in (rising if move > 0 else [count - 1 - k for k in rising])
                    for y in range(self.per)
                ]
                parts.append(lax.ppermute(parts[-1], "row", pairs))
        slots = jnp.stack(up[:0:-1] + [value] + down[1:], axis=0)
        return lax.dynamic_slice_in_dim(slots, count - 1 - self.group, count, axis=0)

    def lanes(self, value):
        value = value[None]
        bit = 1
        while bit < self.per:
            other = self.over_row(value, lambda r: r ^ bit)
            odd = (self.lane // bit) % 2 == 1
            value = jnp.concatenate([jnp.where(odd, other, value), jnp.where(odd, value, other)], axis=0)
            bit *= 2
        return value

    def line_row(self, piece):
        half = piece.shape[0] // 2
        first = jnp.swapaxes(self.line(self.lanes(piece[:half])), 0, 1)
        second = self.lanes(self.line(piece[half:]))
        return jnp.concatenate([first, second], axis=2).reshape(-1, piece.shape[1])

    def first_pieces(self, value):
        size = value.shape[0] // self.cols
        piece = None
        for q in range(self.cols):
            pairs = [
                ((g * self.per + y, 0), (q * self.per + y, g))
                for g in range(self.cols)
                for y in range(self.per)
            ]
            got = self.over_both(value[q * size : (q + 1) * size], pairs)
            piece = got if piece is None else piece + got
        return piece

    def along_row(self, piece):
        whole = lax.all_gather(piece, "row", axis=0).reshape(self.cols, self.per, -1, piece.shape[1])
        return jnp.swapaxes(whole, 0, 1).reshape(-1, piece.shape[1])


def after(value, *others):
    return lax.optimization_barrier((value, *others))[0]


def body(moves_of, matrix):
    moves = moves_of()
    m, n = matrix.shape
    size = m // moves.cols
    at = (moves.row * m + moves.col * size).astype(jnp.int32).reshape(1)
    col_at = (moves.col * n).astype(jnp.int32).reshape(1)
    one, two = BAND, 2 * BAND
    square, tall = (BAND, BAND), (2 * BAND, BAND)

    piece1 = moves.first_pieces(matrix[:, :one])
    raws = moves.deal(after(matrix[:, :two], piece1))
    raw1, raw2 = raws[:, :one], raws[:, one:two]
    raw1_c = after(moves.line_row(piece1), raws)
    gram1, high1, low1 = by_rows(gram_kernel, "gram", n, [col_at, raw1_c], [square, BF16, BF16], 2)
    gram1 = moves.total(gram1)
    heads = moves.spread(raw1_c[one : two + BAND])
    top1, low_head = heads[:BAND], heads[BAND:]
    raw2_c = moves.along_row(moves.first_pieces(after(matrix[:, one:two], high1)))
    part1 = image_of(matrix, high1, low1)
    image1 = moves.scatter_sum(part1)
    inv1 = by_steps(factor_kernel, "factor", gram1)
    y1, x1, mid1 = by_rows(first_kernel, "first", size, [at, raw1, image1, raw2, inv1], [F32, F32, square], 3)
    both = moves.sum_all(jnp.concatenate([mid1, moves.rows_at(x1, one)], axis=0))
    mid1, x1_head = both[:BAND], both[BAND:]
    tm1 = by_steps(transform_kernel, "transform", after(top1, x1), inv1)
    w1, pan2, w1_head, gram2, inner = by_rows(
        second_kernel,
        "second",
        size,
        [at, after(y1, raw2_c), x1, raw2, tm1, mid1, x1_head, top1, inv1],
        [F32, F32, square, square, tall],
        9,
    )
    placed2 = moves.place(pan2)
    pan2_c = moves.along_row(placed2)
    both = moves.sum_all(after(jnp.concatenate([gram2, moves.rows_at(pan2, two)], axis=0), placed2))
    gram2, top2 = both[:BAND], both[BAND:]
    inv2 = by_steps(factor_kernel, "factor", gram2)
    both = moves.sum_all(after(jnp.concatenate([inner, moves.rows_at(w1, two)], axis=0), gram2))
    inner, w1_next = both[: 2 * BAND], both[2 * BAND :]
    pair1 = moves.collect(after(jnp.concatenate([y1, w1], axis=1), inner))
    y1_r, w1_r = pair1[:, :BAND], pair1[:, BAND:]
    raw3 = moves.deal(after(matrix[:, two : two + BAND], placed2))
    ready = after(pan2_c, raw3, inv2)
    high2, low2 = by_rows(halves_kernel, "halves", n, [col_at, ready], [BF16, BF16], 1)
    part2 = image_of(matrix, high2, low2)
    image2 = moves.scatter_sum(part2)
    y1_c, w1_c = by_rows(
        sides_kernel, "sides", n, [col_at, raw1_c, raw2_c, after(pan2_c, part2), inv1, tm1, w1_head], [F32, F32], 3
    )
    tm2 = by_steps(transform_kernel, "transform", top2, inv2)
    x2, y2, mid2 = by_rows(
        next_kernel,
        "next",
        size,
        [at, raw3, y1, w1, w1_next, low_head, inv1, image2, after(inner, tm2), pan2, inv2],
        [F32, F32, square],
        8,
    )
    placed3 = moves.place(x2)
    x2_c = moves.along_row(placed3)
    mid2 = moves.sum_all(after(mid2, placed3))
    half = update(matrix, y1_r, after(w1_r, x2), y1_c, w1_c, "update_first", 3)
    (y2_c,) = by_rows(
        functools.partial(vectors_kernel, two), "vectors", n, [col_at, after(pan2_c, x2), inv2], [F32], 1
    )
    (w2,) = by_rows(last_kernel, "last", size, [y2, x2, tm2, mid2], [F32], 2)
    pair2 = moves.collect(jnp.concatenate([y2, w2], axis=1))
    y2_r, w2_r = pair2[:, :BAND], pair2[:, BAND:]
    (w2_c,) = by_rows(last_kernel, "last", n, [y2_c, x2_c, tm2, mid2], [F32], 2)
    updated = update(half, y2_r, w2_r, y2_c, w2_c, "update_second")
    return updated, jnp.concatenate([y1_r, y2_r], axis=1)


def solution(mesh):
    def run(matrix):
        return body(lambda: Moves(mesh), matrix)

    return jax.shard_map(
        run,
        mesh=mesh,
        in_specs=(P("row", "col"),),
        out_specs=(P("row", "col"), P("row", None)),
        check_vma=False,
    )
```

```python
import functools

import jax
import jax.numpy as jnp
from jax import lax
from jax.experimental import pallas as pl
from jax.experimental.pallas import tpu as pltpu
from jax.sharding import PartitionSpec as P

BAND = 256
NB = 64
EXACT = lax.Precision.HIGHEST


def dot_in(left, right, dims=((1,), (0,))):
    return lax.dot_general(
        left, right, (dims, ((), ())), precision=EXACT, preferred_element_type=jnp.float32
    )


def beside_identity(block):
    size = block.shape[0]
    rows = lax.broadcasted_iota(jnp.int32, (size, size), 0)
    columns = lax.broadcasted_iota(jnp.int32, (size, size), 1)
    return jnp.concatenate([block, (rows == columns).astype(jnp.float32)], axis=1)


def eliminate_below(both):
    size = both.shape[0]
    tiles = [both[8 * i : 8 * i + 8] for i in range(size // 8)]
    place = lax.broadcasted_iota(jnp.int32, (8, 2 * size), 0)
    for k in range(size):
        first, inside = divmod(k, 8)
        row = tiles[first][inside : inside + 1, :]
        scale = lax.rsqrt(row[:, k : k + 1])
        scaled = row * scale
        twice = scaled * scale
        for b in range(first, len(tiles)):
            new = tiles[b] - tiles[b][:, k : k + 1] * twice
            if b == first:
                new = jnp.where(place > inside, new, jnp.where(place == inside, scaled, tiles[b]))
            tiles[b] = new
    return jnp.concatenate(tiles, axis=0)


def eliminate_all(both):
    size = both.shape[0]
    tiles = [both[8 * i : 8 * i + 8] for i in range(size // 8)]
    place = lax.broadcasted_iota(jnp.int32, (8, 2 * size), 0)
    for k in range(size):
        first, inside = divmod(k, 8)
        row = tiles[first][inside : inside + 1, :]
        scaled = row / row[:, k : k + 1]
        new_tiles = []
        for b in range(len(tiles)):
            new = tiles[b] - tiles[b][:, k : k + 1] * scaled
            if b == first:
                new = jnp.where(place == inside, scaled, new)
            new_tiles.append(new)
        tiles = new_tiles
    return jnp.concatenate(tiles, axis=0)


def square_places():
    rows = lax.broadcasted_iota(jnp.int32, (BAND, BAND), 0)
    columns = lax.broadcasted_iota(jnp.int32, (BAND, BAND), 1)
    return rows, columns


def factor_kernel(at, start_ref, out_ref, *scratch):
    work_ref = scratch[0] if scratch else out_ref
    rows, columns = square_places()
    if at == 0:
        work_ref[:, :BAND] = start_ref[...]
        work_ref[:, BAND:] = (rows == columns).astype(jnp.float32)
    else:
        work_ref[...] = start_ref[...]
    end = at + NB
    both = eliminate_below(beside_identity(work_ref[at:end, at:end]))
    strip = dot_in(both[:, NB:], work_ref[at:end, :])
    work_ref[at:end, :] = strip
    if end < BAND:
        work_ref[end:, :] -= dot_in(strip[:, end:BAND], strip, ((0,), (0,)))
    else:
        out_ref[...] = jnp.where(rows >= columns, work_ref[:, BAND:], 0.0)


def transform_kernel(at, *refs):
    if at == 0:
        top_ref, inverse_ref, out_ref = refs
        rows, columns = square_places()
        identity = (rows == columns).astype(jnp.float32)
        work_ref = out_ref
        work_ref[:, :BAND] = identity + dot_in(top_ref[...], inverse_ref[...], ((1,), (1,)))
        work_ref[:, BAND:] = identity
    else:
        start_ref, out_ref = refs[:2]
        work_ref = refs[2] if len(refs) > 2 else out_ref
        work_ref[...] = start_ref[...]
    end = at + NB
    both = eliminate_all(beside_identity(work_ref[at:end, at:end]))
    strip = dot_in(both[:, NB:], work_ref[at:end, :])
    if at > 0:
        work_ref[:at, :] -= dot_in(work_ref[:at, at:end], strip)
    if end < BAND:
        work_ref[end:, :] -= dot_in(work_ref[end:, at:end], strip)
    work_ref[at:end, :] = strip
    if end == BAND:
        out_ref[...] = work_ref[:, BAND:]


def by_steps(kernel, name, *operands):
    for at in range(0, BAND, NB):
        last = at + NB == BAND
        shape = (BAND, BAND) if last else (BAND, 2 * BAND)
        operands = (
            pl.pallas_call(
                functools.partial(kernel, at),
                out_shape=jax.ShapeDtypeStruct(shape, jnp.float32),
                scratch_shapes=[pltpu.VMEM((BAND, 2 * BAND), jnp.float32)] if last else [],
                cost_estimate=pl.CostEstimate(
                    flops=6 * 10**9, bytes_accessed=4 * 10**6, transcendentals=BAND
                ),
                name=name,
            )(*operands),
        )
    return operands[0]


NN, NT, TN = ((1,), (0,)), ((1,), (1,)), ((0,), (0,))
GRANT = 56 * 2**20


def halves(value):
    high = value.astype(jnp.bfloat16)
    return high, (value - high.astype(jnp.float32)).astype(jnp.bfloat16)


def dot1(left, right, dims):
    return lax.dot_general(left, right, (dims, ((), ())), preferred_element_type=jnp.float32)


def dot3(left, right, dims):
    lh, ll = halves(left)
    rh, rl = halves(right)
    return dot1(lh, rh, dims) + (dot1(lh, rl, dims) + dot1(ll, rh, dims))


def places_of(offset_ref, size):
    at = offset_ref[0] + pl.program_id(0) * size
    return at + lax.broadcasted_iota(jnp.int32, (size, BAND), 0)


def unit_of(places, start):
    columns = lax.broadcasted_iota(jnp.int32, places.shape, 1)
    return (places - start == columns).astype(jnp.float32)


def add_to(ref, value):
    @pl.when(pl.program_id(0) == 0)
    def _():
        ref[...] = value

    @pl.when(pl.program_id(0) > 0)
    def _():
        ref[...] += value


def first_kernel(offset_ref, raw_ref, image_ref, next_ref, inv_ref, y_ref, x_ref, mid_ref):
    places = places_of(offset_ref, raw_ref.shape[0])
    panel = jnp.where(places >= BAND, raw_ref[...], 0.0)
    y = dot3(panel, inv_ref[...], NT) + unit_of(places, BAND)
    x = dot3(image_ref[...], inv_ref[...], NT) + next_ref[...]
    y_ref[...] = y
    x_ref[...] = x
    add_to(mid_ref, dot3(y, x, TN))


def curvature(tm_ref, mid_ref):
    return dot3(dot3(tm_ref[...], mid_ref[...], NN), tm_ref[...], NT)


def second_kernel(
    offset_ref, y_ref, x_ref, next_ref, tm_ref, mid_ref, xh_ref, top_ref, inv_ref, w_ref, panel_ref, wh_ref, gram_ref, inner_ref
):
    places = places_of(offset_ref, y_ref.shape[0])
    s = curvature(tm_ref, mid_ref)
    rows, columns = square_places()
    yh = dot3(top_ref[...], inv_ref[...], NT) + (rows == columns).astype(F32)
    wh = dot3(xh_ref[...], tm_ref[...], NT) - 0.5 * dot3(yh, s, NN)
    y = y_ref[...]
    w = dot3(x_ref[...], tm_ref[...], NT) - 0.5 * dot3(y, s, NN)
    w_ref[...] = w
    panel = next_ref[...] - dot3(y, wh, NT) - dot3(w, yh, NT)
    panel_ref[...] = panel
    wh_ref[...] = wh
    panel = jnp.where(places >= 2 * BAND, panel, 0.0)
    add_to(gram_ref, dot_in(panel, panel, TN))
    add_to(inner_ref, jnp.concatenate([dot3(w, panel, TN), dot3(y, panel, TN)], axis=0))


def vectors_kernel(start, offset_ref, panel_ref, inv_ref, y_ref):
    places = places_of(offset_ref, panel_ref.shape[0])
    panel = jnp.where(places >= start, panel_ref[...], 0.0)
    y_ref[...] = dot3(panel, inv_ref[...], NT) + unit_of(places, start)


def halves_kernel(offset_ref, panel_ref, high_ref, low_ref):
    places = places_of(offset_ref, panel_ref.shape[0])
    high_ref[...], low_ref[...] = halves(jnp.where(places >= 2 * BAND, panel_ref[...], 0.0))


def sides_kernel(offset_ref, raw_ref, next_ref, panel_ref, inv_ref, tm_ref, wh_ref, y_ref, w_ref):
    places = places_of(offset_ref, raw_ref.shape[0])
    raw = jnp.where(places >= BAND, raw_ref[...], 0.0)
    y = dot3(raw, inv_ref[...], NT) + unit_of(places, BAND)
    y_ref[...] = y
    w_ref[...] = dot3(next_ref[...] - panel_ref[...] - dot3(y, wh_ref[...], NT), tm_ref[...], NT)


def last_kernel(y_ref, x_ref, tm_ref, mid_ref, w_ref):
    s = curvature(tm_ref, mid_ref)
    w_ref[...] = dot3(x_ref[...], tm_ref[...], NT) - 0.5 * dot3(y_ref[...], s, NN)


def gram_kernel(offset_ref, raw_ref, gram_ref, high_ref, low_ref):
    panel = jnp.where(places_of(offset_ref, raw_ref.shape[0]) >= BAND, raw_ref[...], 0.0)
    high_ref[...], low_ref[...] = halves(panel)
    add_to(gram_ref, dot_in(panel, panel, TN))


def next_kernel(
    offset_ref, raw_ref, y_ref, w_ref, wn_ref, low_ref, inv_ref, image_ref, inner_ref, panel_ref, new_ref, out_ref, v_ref, mid_ref
):
    y, w = y_ref[...], w_ref[...]
    yn = dot3(low_ref[...], inv_ref[...], NT)
    third = raw_ref[...] - dot3(y, wn_ref[...], NT) - dot3(w, yn, NT)
    image = image_ref[...] - dot3(y, inner_ref[:BAND], NN) - dot3(w, inner_ref[BAND:], NN)
    out = dot3(image, new_ref[...], NT) + third
    places = places_of(offset_ref, y.shape[0])
    panel = jnp.where(places >= 2 * BAND, panel_ref[...], 0.0)
    v = dot3(panel, new_ref[...], NT) + unit_of(places, 2 * BAND)
    out_ref[...] = out
    v_ref[...] = v
    add_to(mid_ref, dot3(v, out, TN))


F32, BF16 = jnp.float32, jnp.bfloat16


def by_rows(kernel, name, rows, operands, outs, flops):
    tile = rows // 4 if rows > 1000 and rows % 64 == 0 else rows

    def spec(shape):
        if shape[0] == rows:
            return pl.BlockSpec((tile, shape[1]), lambda i: (i, 0))
        return pl.BlockSpec(shape, lambda i: (0,) * len(shape))

    in_specs = [
        pl.BlockSpec(memory_space=pltpu.SMEM) if v.dtype == jnp.int32 else spec(v.shape) for v in operands
    ]
    shapes = [
        jax.ShapeDtypeStruct(o, F32) if isinstance(o, tuple) else jax.ShapeDtypeStruct((rows, BAND), o)
        for o in outs
    ]
    return pl.pallas_call(
        kernel,
        grid=(rows // tile,),
        in_specs=in_specs,
        out_specs=[spec(shape.shape) for shape in shapes],
        out_shape=shapes,
        compiler_params=pltpu.CompilerParams(vmem_limit_bytes=GRANT),
        cost_estimate=pl.CostEstimate(
            flops=flops * 12 * rows * BAND * BAND, bytes_accessed=4 * rows * BAND * 6, transcendentals=0
        ),
        name=name,
    )(*operands)


def image_kernel(matrix_ref, high_ref, low_ref, out_ref):
    high_panel = high_ref[...]
    both = jnp.concatenate([high_panel, low_ref[...]], axis=1)
    m = matrix_ref.shape[0]
    step = m // 4

    def part(at):
        high, low = halves(matrix_ref[at : at + step, :])
        wide = dot1(high, both, NN)
        return wide[:, :BAND] + (wide[:, BAND:] + dot1(low, high_panel, NN))

    @pl.when(pl.program_id(0) == 0)
    def _():
        for at in range(0, m, step):
            out_ref[at : at + step, :] = part(at)

    @pl.when(pl.program_id(0) > 0)
    def _():
        for at in range(0, m, step):
            out_ref[at : at + step, :] += part(at)


def image_of(matrix, high, low):
    m, n = matrix.shape
    deep = 512 if n % 512 == 0 else 256
    return pl.pallas_call(
        image_kernel,
        grid=(n // deep,),
        in_specs=[
            pl.BlockSpec((m, deep), lambda i: (0, i)),
            pl.BlockSpec((deep, BAND), lambda i: (i, 0)),
            pl.BlockSpec((deep, BAND), lambda i: (i, 0)),
        ],
        out_specs=pl.BlockSpec((m, BAND), lambda i: (0, 0)),
        out_shape=jax.ShapeDtypeStruct((m, BAND), F32),
        compiler_params=pltpu.CompilerParams(vmem_limit_bytes=GRANT),
        cost_estimate=pl.CostEstimate(
            flops=8 * m * n * BAND, bytes_accessed=4 * m * n, transcendentals=0
        ),
        name="image",
    )(matrix, high, low)


def update_kernel(matrix_ref, yr_ref, wr_ref, yc_ref, wc_ref, *rest):
    out_ref, high_ref, low_ref = rest[-3:]

    @pl.when(pl.program_id(0) == 0)
    def _():
        high_ref[:, :BAND], low_ref[:, :BAND] = halves(yr_ref[...])
        high_ref[:, BAND:], low_ref[:, BAND:] = halves(wr_ref[...])

    rh, rl = halves(jnp.concatenate([wc_ref[...], yc_ref[...]], axis=1))
    m = matrix_ref.shape[0]
    step = m // 4
    for at in range(0, m, step):
        part = slice(at, at + step)
        high, low = high_ref[part, :], low_ref[part, :]
        product = dot1(high, rh, NT) + (dot1(high, rl, NT) + dot1(low, rh, NT))
        out_ref[part, :] = matrix_ref[part, :] - product


def update(matrix, y_r, w_r, y_c, w_c, name, parts=1):
    m, n = matrix.shape
    wide = 512 if n % 512 == 0 else n // 9 if n % (9 * 128) == 0 else n
    blocks = n // wide
    parts = parts if blocks % parts == 0 else 1
    each = blocks // parts
    out = None
    for part in range(parts):
        here = functools.partial(lambda first, i: (0, first + i), part * each)
        down = functools.partial(lambda first, i: (first + i, 0), part * each)
        whole = pl.BlockSpec((m, BAND), lambda i: (0, 0), pipeline_mode=pl.Buffered(1))
        specs = [pl.BlockSpec((m, wide), here), whole, whole]
        specs += [pl.BlockSpec((wide, BAND), down)] * 2
        operands = [matrix, y_r, w_r, y_c, w_c]
        if out is not None:
            specs.append(pl.BlockSpec(memory_space=pl.ANY))
            operands.append(out)
        out = pl.pallas_call(
            update_kernel,
            grid=(each,),
            in_specs=specs,
            out_specs=pl.BlockSpec((m, wide), here),
            out_shape=jax.ShapeDtypeStruct((m, n), F32),
            scratch_shapes=[pltpu.VMEM((m, 2 * BAND), BF16)] * 2,
            input_output_aliases={5: 0} if len(operands) > 5 else {},
            compiler_params=pltpu.CompilerParams(vmem_limit_bytes=GRANT),
            cost_estimate=pl.CostEstimate(
                flops=(16 if parts == 1 else 1) * m * n * BAND // parts,
                bytes_accessed=(8 if parts == 1 else 1) * m * n // parts,
                transcendentals=0,
            ),
            name=name,
        )(*operands)
    return out


class Moves:
    def __init__(self, mesh):
        self.rows = mesh.shape["row"]
        self.cols = mesh.shape["col"]
        self.per = self.rows // self.cols
        self.row = lax.axis_index("row")
        self.col = lax.axis_index("col")
        self.group = self.row // self.per
        self.lane = self.row % self.per

    def over_col(self, value, to):
        return lax.ppermute(value, "col", [(c, to(c)) for c in range(self.cols) if to(c) is not None])

    def over_both(self, value, pairs):
        flat = [(a * self.cols + b, d * self.cols + e) for (a, b), (d, e) in pairs]
        return lax.ppermute(value, ("row", "col"), flat)

    def spread(self, value):
        bit = self.cols // 2
        while bit:
            got = self.over_col(value, lambda c: c + bit if c % (2 * bit) == 0 else None)
            value = jnp.where(self.col % (2 * bit) == bit, got, value)
            bit //= 2
        return value

    def total(self, value):
        bit = 1
        while bit < self.cols:
            value = value + self.over_col(value, lambda c: c ^ bit)
            bit *= 2
        return value

    def bits(self):
        return [1 << i for i in range(self.cols.bit_length() - 1)]

    def scatter_sum(self, value):
        bits = self.bits()
        value = value.reshape(*[2] * len(bits), value.shape[0] // self.cols, value.shape[1])
        for bit in bits:
            axis = value.ndim - 3
            odd = (self.col // bit) % 2 == 1
            first = lax.index_in_dim(value, 0, axis, keepdims=False)
            second = lax.index_in_dim(value, 1, axis, keepdims=False)
            keep, give = jnp.where(odd, second, first), jnp.where(odd, first, second)
            value = keep + self.over_col(give, lambda c: c ^ bit)
        return value

    def collect(self, piece):
        for bit in self.bits()[::-1]:
            other = self.over_col(piece, lambda c: c ^ bit)
            odd = (self.col // bit) % 2 == 1
            piece = jnp.stack([jnp.where(odd, other, piece), jnp.where(odd, piece, other)], axis=-3)
        return piece.reshape(-1, piece.shape[-1])

    def over_row(self, value, to):
        return lax.ppermute(value, "row", [(r, to(r)) for r in range(self.rows)])

    def sum_all(self, value):
        half = value.shape[0] // 2
        odd = self.col % 2 == 1
        keep = jnp.where(odd, value[half:], value[:half])
        keep = keep + self.over_col(jnp.where(odd, value[:half], value[half:]), lambda c: c ^ 1)
        for bit in self.bits()[1:]:
            keep = keep + self.over_col(keep, lambda c: c ^ bit)
        for bit in [1 << i for i in range(self.rows.bit_length() - 1)]:
            keep = keep + self.over_row(keep, lambda r: r ^ bit)
        other = self.over_col(keep, lambda c: c ^ 1)
        return jnp.concatenate([jnp.where(odd, other, keep), jnp.where(odd, keep, other)], axis=0)

    def deal(self, value):
        size = value.shape[0] // self.cols
        piece = value[:size]
        for q in range(1, self.cols):
            got = self.over_col(value[q * size : (q + 1) * size], lambda c: q if c == 0 else None)
            piece = jnp.where(self.col == q, got, piece)
        return piece

    def rows_at(self, piece, first):
        size = piece.shape[0]
        mine = (self.row * self.cols + self.col) * size
        padded = jnp.pad(piece, ((BAND, BAND), (0, 0)))
        at = jnp.clip(first - mine + BAND, 0, size + BAND)
        return lax.dynamic_slice_in_dim(padded, at, BAND, axis=0)

    def place(self, piece):
        pairs = [
            ((g * self.per + y, q), (q * self.per + y, g))
            for g in range(self.cols)
            for y in range(self.per)
            for q in range(self.cols)
        ]
        return self.over_both(piece, pairs)

    def line(self, value):
        count = self.cols
        up, down = [value], [value]
        for step in range(count - 1):
            rising = range(step, count - 1)
            for parts, move in ((up, 1), (down, -1)):
                pairs = [
                    (g * self.per + y, (g + move) * self.per + y)
                    for g in (rising if move > 0 else [count - 1 - k for k in rising])
                    for y in range(self.per)
                ]
                parts.append(lax.ppermute(parts[-1], "row", pairs))
        slots = jnp.stack(up[:0:-1] + [value] + down[1:], axis=0)
        return lax.dynamic_slice_in_dim(slots, count - 1 - self.group, count, axis=0)

    def lanes(self, value):
        value = value[None]
        bit = 1
        while bit < self.per:
            other = self.over_row(value, lambda r: r ^ bit)
            odd = (self.lane // bit) % 2 == 1
            value = jnp.concatenate([jnp.where(odd, other, value), jnp.where(odd, value, other)], axis=0)
            bit *= 2
        return value

    def line_row(self, piece):
        half = piece.shape[0] // 2
        first = jnp.swapaxes(self.line(self.lanes(piece[:half])), 0, 1)
        second = self.lanes(self.line(piece[half:]))
        return jnp.concatenate([first, second], axis=2).reshape(-1, piece.shape[1])

    def first_pieces(self, value):
        size = value.shape[0] // self.cols
        piece = None
        for q in range(self.cols):
            pairs = [
                ((g * self.per + y, 0), (q * self.per + y, g))
                for g in range(self.cols)
                for y in range(self.per)
            ]
            got = self.over_both(value[q * size : (q + 1) * size], pairs)
            piece = got if piece is None else piece + got
        return piece

    def along_row(self, piece):
        whole = lax.all_gather(piece, "row", axis=0).reshape(self.cols, self.per, -1, piece.shape[1])
        return jnp.swapaxes(whole, 0, 1).reshape(-1, piece.shape[1])


def after(value, *others):
    return lax.optimization_barrier((value, *others))[0]


def body(moves_of, matrix):
    moves = moves_of()
    m, n = matrix.shape
    size = m // moves.cols
    at = (moves.row * m + moves.col * size).astype(jnp.int32).reshape(1)
    col_at = (moves.col * n).astype(jnp.int32).reshape(1)
    one, two = BAND, 2 * BAND
    square, tall = (BAND, BAND), (2 * BAND, BAND)

    piece1 = moves.first_pieces(matrix[:, :one])
    raws = moves.deal(after(matrix[:, :two], piece1))
    raw1, raw2 = raws[:, :one], raws[:, one:two]
    raw1_c = after(moves.line_row(piece1), raws)
    gram1, high1, low1 = by_rows(gram_kernel, "gram", n, [col_at, raw1_c], [square, BF16, BF16], 2)
    gram1 = moves.total(gram1)
    heads = moves.spread(raw1_c[one : two + BAND])
    top1, low_head = heads[:BAND], heads[BAND:]
    raw2_c = moves.along_row(moves.first_pieces(after(matrix[:, one:two], high1)))
    part1 = image_of(matrix, high1, low1)
    image1 = moves.scatter_sum(part1)
    inv1 = by_steps(factor_kernel, "factor", gram1)
    y1, x1, mid1 = by_rows(first_kernel, "first", size, [at, raw1, image1, raw2, inv1], [F32, F32, square], 3)
    both = moves.sum_all(jnp.concatenate([mid1, moves.rows_at(x1, one)], axis=0))
    mid1, x1_head = both[:BAND], both[BAND:]
    y1_r = moves.collect(after(y1, x1_head))
    tm1 = by_steps(transform_kernel, "transform", after(top1, x1), inv1)
    w1, pan2, w1_head, gram2, inner = by_rows(
        second_kernel,
        "second",
        size,
        [at, after(y1, raw2_c), x1, raw2, tm1, mid1, x1_head, top1, inv1],
        [F32, F32, square, square, tall],
        9,
    )
    placed2 = moves.place(pan2)
    pan2_c = moves.along_row(placed2)
    both = moves.sum_all(after(jnp.concatenate([gram2, moves.rows_at(pan2, two)], axis=0), placed2))
    gram2, top2 = both[:BAND], both[BAND:]
    raw3 = moves.deal(after(matrix[:, two : two + BAND], placed2))
    ready = after(pan2_c, raw3)
    high2, low2 = by_rows(halves_kernel, "halves", n, [col_at, ready], [BF16, BF16], 1)
    both = moves.sum_all(after(jnp.concatenate([inner, moves.rows_at(w1, two)], axis=0), high2))
    inner, w1_next = both[: 2 * BAND], both[2 * BAND :]
    w1_r = moves.collect(after(w1, high2))
    part2 = image_of(matrix, high2, low2)
    inv2 = by_steps(factor_kernel, "factor", after(gram2, part2))
    image2 = moves.scatter_sum(part2)
    x2, y2, mid2 = by_rows(
        next_kernel,
        "next",
        size,
        [at, raw3, y1, w1, w1_next, low_head, inv1, image2, inner, pan2, inv2],
        [F32, F32, square],
        8,
    )
    placed3 = moves.place(x2)
    x2_c = moves.along_row(placed3)
    y1_c, w1_c = by_rows(
        sides_kernel, "sides", n, [col_at, raw1_c, raw2_c, after(pan2_c, x2), inv1, tm1, w1_head], [F32, F32], 1
    )
    mid2 = moves.sum_all(after(mid2, placed3))
    pair2 = moves.collect(after(jnp.concatenate([y2, x2], axis=1), placed3))
    y2_r, x2_r = pair2[:, :BAND], pair2[:, BAND:]
    half = update(matrix, y1_r, after(w1_r, x2), y1_c, w1_c, "update_first", 3)
    tm2 = by_steps(transform_kernel, "transform", after(top2, half), inv2)
    (y2_c,) = by_rows(
        functools.partial(vectors_kernel, two), "vectors", n, [col_at, after(pan2_c, x2), inv2], [F32], 1
    )
    (w2_r,) = by_rows(last_kernel, "last", m, [y2_r, x2_r, tm2, mid2], [F32], 2)
    (w2_c,) = by_rows(last_kernel, "last", n, [y2_c, x2_c, tm2, mid2], [F32], 2)
    updated = update(half, y2_r, w2_r, y2_c, w2_c, "update_second")
    return updated, jnp.concatenate([y1_r, y2_r], axis=1)


def solution(mesh):
    def run(matrix):
        return body(lambda: Moves(mesh), matrix)

    return jax.shard_map(
        run,
        mesh=mesh,
        in_specs=(P("row", "col"),),
        out_specs=(P("row", "col"), P("row", None)),
        check_vma=False,
    )
```
